256 devices in a mesh: dp: 32 (over x, y, core), tensor: 8 (over z).
Axes of the slice: x: 4, y: 4, z: 8, core: 2. Of those that a mesh axis runs over, the one named last changes fastest.
Arguments:
- activations: bfloat16 [32768, 8192], P(('dp', 'tensor')), may hold values from -24 to 24
- out_grads: bfloat16 [32768, 2048], P('dp', 'tensor'), may hold values from -0.059814453 to 0.059814453
- master: float32 [8192, 2048], P('dp', 'tensor'), may hold values from -3 to 3
- first_moment: float32 [8192, 2048], P('dp', 'tensor'), may hold values from -2 to 2
- second_moment: float32 [8192, 2048], P('dp', 'tensor'), may hold values from 0.01 to 1
Outputs:
- new_master: float32 [8192, 2048], P('dp', 'tensor')
- new_first: float32 [8192, 2048], P('dp', 'tensor')
- new_second: float32 [8192, 2048], P('dp', 'tensor')
- weights: bfloat16 [8192, 2048], P(None, 'tensor')
The draws below stay inside these ranges and needn't reach their ends.
All inputs are finite; a program needn't handle non-finite values.
Results may differ from the reference program's by a relative error of at most 0.013.
Values may be sent and summed in bfloat16 or wider, within the bound.
No kernel may reach another device: no remote copies, remote signals or barrier semaphores. Data moves between devices by JAX's collectives and lax.ppermute only.
A program may use at most 128 MiB of HBM per device.

```python
import math
import jax
import jax.numpy as jnp

D = 8192
TOKENS = 32768
COLS = 2048


def strengthened(array, stream_key, source, target, blocks, factor):
    def block_of(axis_at):
        return (jnp.arange(array.shape[axis_at]) // (array.shape[axis_at] // blocks)).reshape((-1,) + (1,) * (array.ndim - 1 - axis_at))

    near = jax.random.permutation(stream_key, blocks)[block_of(target)]
    far = (block_of(target) + blocks // 2) % blocks
    return jnp.where((block_of(source) == near) | (block_of(source) == far), factor * array, array)


def shard_levels(rng, shape, shards, least, largest):
    def one(axis_at, parts):
        heights = jax.random.uniform(jax.random.fold_in(jax.random.fold_in(rng, 6), axis_at), (parts,), jnp.float32, least / len(shards), largest / len(shards))
        return jnp.repeat(jnp.exp(heights), shape[axis_at] // parts).reshape((-1,) + (1,) * (len(shape) - axis_at - 1))

    loudness = one(*shards[0])
    for cut in shards[1:]:
        loudness = loudness * one(*cut)
    return loudness


def normal_values(own_key, dims, width, limit, cuts=(), kind=jnp.bfloat16):
    values = width * jax.random.normal(own_key, dims, jnp.float32)
    if cuts:
        values = values * shard_levels(own_key, dims, cuts, -0.22, 0.18)
    return jnp.clip(values, -limit, limit).astype(kind)


def heavy_noise(rng, dims, deviation, most, split, heavy, held_as=jnp.bfloat16):
    result = deviation * jax.random.normal(rng, dims, jnp.float32)
    if split:
        result = result * shard_levels(rng, dims, split, -0.22, 0.18)
    return jnp.clip(strengthened(result, jax.random.fold_in(rng, 3), *heavy), -most, most).astype(held_as)


def setup_inputs(seed: int = 0) -> dict:
    key_list = jax.random.split(jax.random.key(seed), 6)
    activations = heavy_noise(key_list[0], (TOKENS, D), 1.0, 24.0, ((0, 256),), (0, 1, 256, 6.0))
    out_grads = normal_values(key_list[1], (TOKENS, COLS), 0.01, 0.059814453, ((0, 32), (1, 8)))
    master = normal_values(key_list[2], (D, COLS), 0.5, 3.0, ((0, 32), (1, 8)), jnp.float32)
    first_moment = normal_values(key_list[3], (D, COLS), 0.3, 2.0, ((0, 32), (1, 8)), jnp.float32)
    second_moment = jnp.clip(jnp.exp(math.log(1.0) - 4.6051702 * jax.random.uniform(key_list[4], (D, COLS), jnp.float32) ** shard_levels(key_list[4], (D, COLS), ((0, 32), (1, 8)), -0.2, 0.2)), 0.01, 1.0)
    return dict(activations=activations, out_grads=out_grads, master=master, first_moment=first_moment, second_moment=second_moment)


first_bias = 0.9999734386011124
second_bias = 0.0952078528862911

def reference(activations, out_grads, master, first_moment, second_moment):
    grad = jnp.dot(activations.T, out_grads, preferred_element_type=jnp.float32)
    new_first = 0.9 * first_moment + 0.1 * grad
    new_second = 0.999 * second_moment + 0.001 * grad * grad
    first_fix = new_first / first_bias
    second_fix = new_second / second_bias
    new_master = master * (1.0 - 0.05 * 0.1) - 0.05 * first_fix / (jnp.sqrt(second_fix) + 1e-08)
    return (new_master, new_first, new_second, new_master.astype(jnp.bfloat16))
```

```python
import functools

import jax
import jax.numpy as jnp
from jax import lax
from jax.experimental import pallas as pl
from jax.experimental.pallas import tpu as pltpu
from jax.sharding import PartitionSpec as P

first_bias = 0.9999734386011124
second_bias = 0.0952078528862911

SIDE = 4


def device_at(x, y, core):
    return ((x % SIDE) * SIDE + (y % SIDE)) * 2 + core


PLACES = [(x, y, core) for x in range(SIDE) for y in range(SIDE) for core in range(2)]
CORE_SWAP = [(device_at(x, y, core), device_at(x, y, 1 - core)) for x, y, core in PLACES]


def ring(step, along_x_on):
    return [
        (
            device_at(x, y, core),
            device_at(x + step, y, core) if core == along_x_on else device_at(x, y + step, core),
        )
        for x, y, core in PLACES
    ]


def groups(along_x_on):
    lines = []
    for at in range(SIDE):
        lines.append([device_at(i, at, along_x_on) for i in range(SIDE)])
        lines.append([device_at(at, i, 1 - along_x_on) for i in range(SIDE)])
    return lines


def place():
    dp = lax.axis_index("dp")
    return dp // (2 * SIDE), (dp // 2) % SIDE, dp % 2


def block_of(x, y, core, split, reduce):
    first = core == 0
    bx = lax.rem(x + jnp.where(first, split, reduce), SIDE)
    by = lax.rem(y + jnp.where(first, reduce, split), SIDE)
    return (bx * SIDE + by) * 2 + core


def run_copies(copies):
    for copy in copies:
        copy.start()
    for copy in copies:
        copy.wait()


def for_peer_kernel(rows, acts, out, sem):
    x, y, core = place()
    copies = []
    for split in range(SIDE):
        for reduce in range(SIDE):
            block = block_of(x, y, 1 - core, split, reduce)
            copies.append(
                pltpu.make_async_copy(
                    acts.at[:, pl.ds(pl.multiple_of(block * rows, rows), rows)],
                    out.at[split, :, pl.ds(reduce * rows, rows)],
                    sem.at[split * SIDE + reduce],
                )
            )
    run_copies(copies)


def chunks_kernel(rows, acts, peer, *rest):
    outs, sem = rest[:SIDE], rest[SIDE]
    x, y, core = place()
    copies = []
    for split in range(SIDE):
        for reduce in range(SIDE):
            block = block_of(x, y, core, split, reduce)
            copies.append(
                pltpu.make_async_copy(
                    acts.at[:, pl.ds(pl.multiple_of(block * rows, rows), rows)],
                    outs[split].at[0, :, pl.ds(reduce * rows, rows)],
                    sem.at[split * SIDE + reduce],
                )
            )
        copies.append(
            pltpu.make_async_copy(peer.at[split], outs[split].at[1], sem.at[SIDE * SIDE + split])
        )
    run_copies(copies)


def product_kernel(rows, a0, a1, a2, a3, g0, g1, g2, g3, out, turned):
    tokens = a0.shape[1]

    @pl.when(pl.program_id(0) == 0)
    def _():
        for i, piece in enumerate((a0, a1, a2, a3)):
            for core in range(2):
                at = (2 * i + core) * tokens
                turned[:, at : at + tokens] = piece[core].T

    right = jnp.concatenate([piece[core, 0] for piece in (g0, g1, g2, g3) for core in range(2)], axis=0)
    for reduce in range(SIDE):
        out[reduce, 0] = jnp.dot(
            turned[reduce * rows : (reduce + 1) * rows, :], right, preferred_element_type=jnp.float32
        ).astype(out.dtype)


def weights_kernel(rows, own, peer, out, sem):
    _, _, core = place()
    copies = []
    for which, (array, of_core) in enumerate(((own, core), (peer, 1 - core))):
        for i in range(SIDE):
            for j in range(SIDE):
                block = jnp.where(of_core == 0, j * SIDE + i, i * SIDE + j) * 2 + of_core
                copies.append(
                    pltpu.make_async_copy(
                        array.at[i, j],
                        out.at[pl.ds(pl.multiple_of(block * rows, rows), rows), :],
                        sem.at[(which * SIDE + i) * SIDE + j],
                    )
                )
    run_copies(copies)


ANY = pl.BlockSpec(memory_space=pl.ANY)


def mover(kernel, out_shape, count, inputs):
    return pl.pallas_call(
        kernel,
        out_shape=out_shape,
        in_specs=[ANY] * inputs,
        out_specs=jax.tree.map(lambda _: ANY, out_shape),
        scratch_shapes=[pltpu.SemaphoreType.DMA((count,))],
    )


def per_device(activations, out_grads, master, first_moment, second_moment):
    tokens, width = activations.shape
    rows, cols = master.shape
    panels = out_grads.shape[0] // tokens
    kept = jax.ShapeDtypeStruct
    wide = SIDE * rows

    for_peer = mover(
        functools.partial(for_peer_kernel, rows), kept((SIDE, tokens, wide), jnp.bfloat16), SIDE * SIDE, 1
    )(activations)
    from_peer = lax.ppermute(for_peer, "dp", CORE_SWAP)
    chunk = kept((2, tokens, wide), jnp.bfloat16)
    chunks = mover(
        functools.partial(chunks_kernel, rows), [chunk] * SIDE, SIDE * SIDE + SIDE, 2
    )(activations, from_peer)
    acts = [chunks[0]] + [lax.ppermute(chunks[i], "dp", ring(i, 0)) for i in range(1, SIDE)]

    mine = lax.all_to_all(out_grads.reshape(panels, tokens, cols), "tensor", 0, 0)
    both = jnp.stack([mine, lax.ppermute(mine, "dp", CORE_SWAP)])
    grads = [both] + [lax.ppermute(both, "dp", ring(i, 0)) for i in range(1, SIDE)]

    parts = pl.pallas_call(
        functools.partial(product_kernel, rows),
        grid=(panels,),
        out_shape=kept((SIDE, panels, rows, cols), jnp.bfloat16),
        in_specs=[pl.BlockSpec((2, tokens, wide), lambda i: (0, 0, 0))] * SIDE
        + [pl.BlockSpec((2, 1, tokens, cols), lambda i: (0, i, 0, 0))] * SIDE,
        out_specs=pl.BlockSpec((SIDE, 1, rows, cols), lambda i: (0, i, 0, 0)),
        scratch_shapes=[pltpu.VMEM((wide, 2 * SIDE * tokens), jnp.bfloat16)],
        compiler_params=pltpu.CompilerParams(vmem_limit_bytes=40 * 1024 * 1024),
    )(*acts, *grads)

    half = panels // 2
    f32 = jnp.float32
    up = lax.ppermute(parts[2, :half], "dp", ring(1, 1))
    down = lax.ppermute(parts[2, half:], "dp", ring(3, 1))
    up_sum = (parts[1, :half].astype(f32) + up.astype(f32)).astype(jnp.bfloat16)
    down_sum = (parts[3, half:].astype(f32) + down.astype(f32)).astype(jnp.bfloat16)
    up = lax.ppermute(jnp.concatenate([up_sum, parts[1, half:]]), "dp", ring(1, 1))
    down = lax.ppermute(jnp.concatenate([parts[3, :half], down_sum]), "dp", ring(3, 1))
    line = (parts[0].astype(f32) + up.astype(f32) + down.astype(f32)).astype(jnp.bfloat16)

    grad = jnp.sum(lax.all_to_all(line, "tensor", 0, 0).astype(f32), axis=0)

    new_first = 0.9 * first_moment + 0.1 * grad
    new_second = 0.999 * second_moment + 0.001 * grad * grad
    first_fix = new_first / first_bias
    second_fix = new_second / second_bias
    new_master = master * (1.0 - 0.05 * 0.1) - 0.05 * first_fix / (jnp.sqrt(second_fix) + 1e-08)

    own = new_master.astype(jnp.bfloat16)
    own = lax.all_to_all(
        jnp.broadcast_to(own, (SIDE, rows, cols)), "dp", 0, 0, axis_index_groups=groups(0)
    )
    own = lax.all_to_all(
        jnp.broadcast_to(own, (SIDE, SIDE, rows, cols)), "dp", 0, 0, axis_index_groups=groups(1)
    )
    peer = lax.ppermute(own, "dp", CORE_SWAP)
    weights = mover(
        functools.partial(weights_kernel, rows), kept((width, cols), jnp.bfloat16), 2 * SIDE * SIDE, 2
    )(own, peer)
    return (new_master, new_first, new_second, weights)


def solution(mesh):
    return jax.shard_map(
        per_device,
        mesh=mesh,
        in_specs=(
            P(("dp", "tensor"), None),
            P("dp", "tensor"),
            P("dp", "tensor"),
            P("dp", "tensor"),
            P("dp", "tensor"),
        ),
        out_specs=(P("dp", "tensor"), P("dp", "tensor"), P("dp", "tensor"), P(None, "tensor")),
        check_vma=False,
    )
```

```python
import functools

import jax
import jax.numpy as jnp
from jax import lax
from jax.experimental import pallas as pl
from jax.experimental.pallas import tpu as pltpu
from jax.sharding import PartitionSpec as P

first_bias = 0.9999734386011124
second_bias = 0.0952078528862911

SIDE = 4


def device_at(x, y, core):
    return ((x % SIDE) * SIDE + (y % SIDE)) * 2 + core


PLACES = [(x, y, core) for x in range(SIDE) for y in range(SIDE) for core in range(2)]
CORE_SWAP = [(device_at(x, y, core), device_at(x, y, 1 - core)) for x, y, core in PLACES]


def ring(step, along_x_on):
    return [
        (
            device_at(x, y, core),
            device_at(x + step, y, core) if core == along_x_on else device_at(x, y + step, core),
        )
        for x, y, core in PLACES
    ]


def groups(along_x_on):
    lines = []
    for at in range(SIDE):
        lines.append([device_at(i, at, along_x_on) for i in range(SIDE)])
        lines.append([device_at(at, i, 1 - along_x_on) for i in range(SIDE)])
    return lines


def place():
    dp = lax.axis_index("dp")
    return dp // (2 * SIDE), (dp // 2) % SIDE, dp % 2


def block_of(x, y, core, split, reduce):
    first = core == 0
    bx = lax.rem(x + jnp.where(first, split, reduce), SIDE)
    by = lax.rem(y + jnp.where(first, reduce, split), SIDE)
    return (bx * SIDE + by) * 2 + core


def block_at(array, block, rows):
    return array[:, pl.ds(pl.multiple_of(block * rows, rows), rows)]


def for_peer_kernel(rows, acts, out):
    x, y, core = place()
    for split in range(SIDE):
        for reduce in range(SIDE):
            block = block_of(x, y, 1 - core, split, reduce)
            out[split, :, reduce * rows : (reduce + 1) * rows] = block_at(acts, block, rows)


def chunks_kernel(rows, acts, peer, *outs):
    x, y, core = place()
    for split in range(SIDE):
        for reduce in range(SIDE):
            block = block_of(x, y, core, split, reduce)
            outs[split][0, :, reduce * rows : (reduce + 1) * rows] = block_at(acts, block, rows)
        outs[split][1] = peer[split]


def product_kernel(rows, a0, a1, a2, a3, g0, g1, g2, g3, out, turned):
    tokens = a0.shape[1]

    @pl.when(pl.program_id(0) == 0)
    def _():
        for i, piece in enumerate((a0, a1, a2, a3)):
            for core in range(2):
                at = (2 * i + core) * tokens
                turned[:, at : at + tokens] = piece[core].T

    right = jnp.concatenate([piece[core, 0] for piece in (g0, g1, g2, g3) for core in range(2)], axis=0)
    for reduce in range(SIDE):
        out[reduce, 0] = jnp.dot(
            turned[reduce * rows : (reduce + 1) * rows, :], right, preferred_element_type=jnp.float32
        ).astype(out.dtype)


def weights_kernel(own, peer, out):
    _, _, core = place()
    x = pl.program_id(0)
    for of_core, (first, second) in enumerate(((own, peer), (peer, own))):

        @pl.when(core == of_core)
        def _():
            for y in range(SIDE):
                out[0, y, 0] = first[y, x]
                out[0, y, 1] = second[x, y]


VMEM = pl.BlockSpec(memory_space=pltpu.VMEM)


def mover(kernel, out_shape, inputs):
    return pl.pallas_call(
        kernel,
        out_shape=out_shape,
        in_specs=[VMEM] * inputs,
        out_specs=jax.tree.map(lambda _: VMEM, out_shape),
        compiler_params=pltpu.CompilerParams(vmem_limit_bytes=32 * 1024 * 1024),
    )


def per_device(activations, out_grads, master, first_moment, second_moment):
    tokens, width = activations.shape
    rows, cols = master.shape
    panels = out_grads.shape[0] // tokens
    kept = jax.ShapeDtypeStruct
    wide = SIDE * rows

    for_peer = mover(
        functools.partial(for_peer_kernel, rows), kept((SIDE, tokens, wide), jnp.bfloat16), 1
    )(activations)
    from_peer = lax.ppermute(for_peer, "dp", CORE_SWAP)
    chunk = kept((2, tokens, wide), jnp.bfloat16)
    chunks = mover(
        functools.partial(chunks_kernel, rows), [chunk] * SIDE, 2
    )(activations, from_peer)
    acts = [chunks[0]] + [lax.ppermute(chunks[i], "dp", ring(i, 0)) for i in range(1, SIDE)]

    mine = lax.all_to_all(out_grads.reshape(panels, tokens, cols), "tensor", 0, 0)
    both = jnp.stack([mine, lax.ppermute(mine, "dp", CORE_SWAP)])
    grads = [both] + [lax.ppermute(both, "dp", ring(i, 0)) for i in range(1, SIDE)]

    parts = pl.pallas_call(
        functools.partial(product_kernel, rows),
        grid=(panels,),
        out_shape=kept((SIDE, panels, rows, cols), jnp.bfloat16),
        in_specs=[pl.BlockSpec((2, tokens, wide), lambda i: (0, 0, 0))] * SIDE
        + [pl.BlockSpec((2, 1, tokens, cols), lambda i: (0, i, 0, 0))] * SIDE,
        out_specs=pl.BlockSpec((SIDE, 1, rows, cols), lambda i: (0, i, 0, 0)),
        scratch_shapes=[pltpu.VMEM((wide, 2 * SIDE * tokens), jnp.bfloat16)],
        compiler_params=pltpu.CompilerParams(vmem_limit_bytes=40 * 1024 * 1024),
    )(*acts, *grads)

    half = panels // 2
    f32 = jnp.float32
    up = lax.ppermute(parts[2, :half], "dp", ring(1, 1))
    down = lax.ppermute(parts[2, half:], "dp", ring(3, 1))
    up_sum = (parts[1, :half].astype(f32) + up.astype(f32)).astype(jnp.bfloat16)
    down_sum = (parts[3, half:].astype(f32) + down.astype(f32)).astype(jnp.bfloat16)
    up = lax.ppermute(jnp.concatenate([up_sum, parts[1, half:]]), "dp", ring(1, 1))
    down = lax.ppermute(jnp.concatenate([parts[3, :half], down_sum]), "dp", ring(3, 1))
    line = (parts[0].astype(f32) + up.astype(f32) + down.astype(f32)).astype(jnp.bfloat16)

    grad = jnp.sum(lax.all_to_all(line, "tensor", 0, 0).astype(f32), axis=0)

    new_first = 0.9 * first_moment + 0.1 * grad
    new_second = 0.999 * second_moment + 0.001 * grad * grad
    first_fix = new_first / first_bias
    second_fix = new_second / second_bias
    new_master = master * (1.0 - 0.05 * 0.1) - 0.05 * first_fix / (jnp.sqrt(second_fix) + 1e-08)

    own = new_master.astype(jnp.bfloat16)
    own = lax.all_to_all(
        jnp.broadcast_to(own, (SIDE, rows, cols)), "dp", 0, 0, axis_index_groups=groups(0)
    )
    own = lax.all_to_all(
        jnp.broadcast_to(own, (SIDE, SIDE, rows, cols)), "dp", 0, 0, axis_index_groups=groups(1)
    )
    peer = lax.ppermute(own, "dp", CORE_SWAP)
    weights = pl.pallas_call(
        weights_kernel,
        grid=(SIDE,),
        out_shape=kept((SIDE, SIDE, 2, rows, cols), jnp.bfloat16),
        in_specs=[VMEM] * 2,
        out_specs=pl.BlockSpec((1, SIDE, 2, rows, cols), lambda i: (i, 0, 0, 0, 0)),
        compiler_params=pltpu.CompilerParams(vmem_limit_bytes=32 * 1024 * 1024),
    )(own, peer).reshape(width, cols)
    return (new_master, new_first, new_second, weights)


def solution(mesh):
    return jax.shard_map(
        per_device,
        mesh=mesh,
        in_specs=(
            P(("dp", "tensor"), None),
            P("dp", "tensor"),
            P("dp", "tensor"),
            P("dp", "tensor"),
            P("dp", "tensor"),
        ),
        out_specs=(P("dp", "tensor"), P("dp", "tensor"), P("dp", "tensor"), P(None, "tensor")),
        check_vma=False,
    )
```

```python
import functools

import jax
import jax.numpy as jnp
from jax import lax
from jax.experimental import pallas as pl
from jax.experimental.pallas import tpu as pltpu
from jax.sharding import PartitionSpec as P

first_bias = 0.9999734386011124
second_bias = 0.0952078528862911

SIDE = 4


def device_at(x, y, core):
    return ((x % SIDE) * SIDE + (y % SIDE)) * 2 + core


PLACES = [(x, y, core) for x in range(SIDE) for y in range(SIDE) for core in range(2)]
CORE_SWAP = [(device_at(x, y, core), device_at(x, y, 1 - core)) for x, y, core in PLACES]


def ring(step, along_x_on):
    return [
        (
            device_at(x, y, core),
            device_at(x + step, y, core) if core == along_x_on else device_at(x, y + step, core),
        )
        for x, y, core in PLACES
    ]


def groups(along_x_on):
    lines = []
    for at in range(SIDE):
        lines.append([device_at(i, at, along_x_on) for i in range(SIDE)])
        lines.append([device_at(at, i, 1 - along_x_on) for i in range(SIDE)])
    return lines


def place():
    dp = lax.axis_index("dp")
    return dp // (2 * SIDE), (dp // 2) % SIDE, dp % 2


def block_of(x, y, core, split, reduce):
    first = core == 0
    bx = lax.rem(x + jnp.where(first, split, reduce), SIDE)
    by = lax.rem(y + jnp.where(first, reduce, split), SIDE)
    return (bx * SIDE + by) * 2 + core


def block_at(array, block, rows):
    return array[:, pl.ds(pl.multiple_of(block * rows, rows), rows)]


def for_peer_kernel(rows, acts, out):
    x, y, core = place()
    for split in range(SIDE):
        for reduce in range(SIDE):
            block = block_of(x, y, 1 - core, split, reduce)
            out[split, :, reduce * rows : (reduce + 1) * rows] = block_at(acts, block, rows)


def chunks_kernel(rows, acts, peer, *outs):
    x, y, core = place()
    for split in range(SIDE):
        for reduce in range(SIDE):
            block = block_of(x, y, core, split, reduce)
            outs[split][0, :, reduce * rows : (reduce + 1) * rows] = block_at(acts, block, rows)
        outs[split][1] = peer[split]


def product_kernel(which, rows, a0, a1, a2, a3, g0, g1, g2, g3, *outs):
    acts, grads = (a0, a1, a2, a3), (g0, g1, g2, g3)
    panels = g0.shape[1]
    here = lax.axis_index("tensor")
    left = {
        reduce: jnp.concatenate(
            [piece[core, :, reduce * rows : (reduce + 1) * rows].T for piece in acts for core in range(2)], axis=1
        )
        for reduce in sorted({reduce for reduce, _ in which})
    }
    for (reduce, away), out in zip(which, outs):
        for i, step in enumerate(away):
            panel = lax.rem(here + step, panels)
            right = jnp.concatenate([piece[core, panel] for piece in grads for core in range(2)], axis=0)
            out[i] = jnp.dot(left[reduce], right, preferred_element_type=jnp.float32).astype(out.dtype)


def weights_kernel(*refs):
    *parts, out = refs
    x, y, core = place()
    panel_x = pl.program_id(0)
    off_x = lax.rem(x + SIDE - panel_x, SIDE)
    for of_core in range(2):
        first, second = parts[SIDE * of_core :][:SIDE], parts[SIDE * (1 - of_core) :][:SIDE]

        for case in range(SIDE):

            @pl.when((core == of_core) & (y == case))
            def _():
                for at in range(SIDE):
                    out[0, at, 0] = first[(case - at) % SIDE][off_x]

            @pl.when((core == of_core) & (off_x == case))
            def _():
                for at in range(SIDE):
                    out[0, at, 1] = second[case][lax.rem(y + SIDE - at, SIDE)]


VMEM = pl.BlockSpec(memory_space=pltpu.VMEM)


def mover(kernel, out_shape, inputs):
    return pl.pallas_call(
        kernel,
        out_shape=out_shape,
        in_specs=[VMEM] * inputs,
        out_specs=jax.tree.map(lambda _: VMEM, out_shape),
        compiler_params=pltpu.CompilerParams(vmem_limit_bytes=20 * 1024 * 1024),
    )


def per_device(activations, out_grads, master, first_moment, second_moment):
    tokens, width = activations.shape
    rows, cols = master.shape
    panels = out_grads.shape[0] // tokens
    kept = jax.ShapeDtypeStruct
    wide = SIDE * rows

    for_peer = mover(
        functools.partial(for_peer_kernel, rows), kept((SIDE, tokens, wide), jnp.bfloat16), 1
    )(activations)
    from_peer = lax.ppermute(for_peer, "dp", CORE_SWAP)
    chunk = kept((2, tokens, wide), jnp.bfloat16)
    chunks = mover(
        functools.partial(chunks_kernel, rows), [chunk] * SIDE, 2
    )(activations, from_peer)
    acts = [chunks[0]] + [lax.ppermute(chunks[i], "dp", ring(i, 0)) for i in range(1, SIDE)]

    mine = lax.all_to_all(out_grads.reshape(panels, tokens, cols), "tensor", 0, 0)
    both = jnp.stack([mine, lax.ppermute(mine, "dp", CORE_SWAP)])
    grads = [both] + [lax.ppermute(both, "dp", ring(i, 0)) for i in range(1, SIDE)]

    def product(*which):
        return mover(
            functools.partial(product_kernel, which, rows),
            [kept((len(away), rows, cols), jnp.bfloat16) for _, away in which],
            2 * SIDE,
        )(*acts, *grads)

    far = tuple(range(panels // 2 - 1, panels // 2 + 2))
    near = tuple(step for step in range(panels) if step not in far)
    f32 = jnp.float32
    moved = [
        [lax.ppermute(part, "dp", ring(i, 1)) for i, part in zip((2, 1, 3), product((2, away), (1, away), (3, away)))]
        for away in (far, near)
    ]
    kept_parts = product((0, far), (0, near))

    def line(at):
        return sum((part.astype(f32) for part in moved[at]), kept_parts[at].astype(f32)).astype(jnp.bfloat16)

    def along_tensor(part, step):
        return lax.ppermute(part, "tensor", [(i, (i + step) % panels) for i in range(panels)])

    line_far = line(0)
    terms = [along_tensor(line_far[i], step) for i, step in enumerate(far)]
    line_near = line(1)
    terms += [along_tensor(line_near[i], step) for i, step in enumerate(near) if step]
    grad = sum((term.astype(f32) for term in terms), line_near[0].astype(f32))

    new_first = 0.9 * first_moment + 0.1 * grad
    new_second = 0.999 * second_moment + 0.001 * grad * grad
    first_fix = new_first / first_bias
    second_fix = new_second / second_bias
    new_master = master * (1.0 - 0.05 * 0.1) - 0.05 * first_fix / (jnp.sqrt(second_fix) + 1e-08)

    own = new_master.astype(jnp.bfloat16)
    line = jnp.stack([own] + [lax.ppermute(own, "dp", ring(i, 0)) for i in range(1, SIDE)])
    own = [line] + [lax.ppermute(line, "dp", ring(i, 1)) for i in range(1, SIDE)]
    peer = [lax.ppermute(part, "dp", CORE_SWAP) for part in own]
    weights = pl.pallas_call(
        weights_kernel,
        grid=(SIDE,),
        out_shape=kept((SIDE, SIDE, 2, rows, cols), jnp.bfloat16),
        in_specs=[VMEM] * (2 * SIDE),
        out_specs=pl.BlockSpec((1, SIDE, 2, rows, cols), lambda i: (i, 0, 0, 0, 0)),
        compiler_params=pltpu.CompilerParams(vmem_limit_bytes=20 * 1024 * 1024),
    )(*own, *peer).reshape(width, cols)
    return (new_master, new_first, new_second, weights)


def solution(mesh):
    return jax.shard_map(
        per_device,
        mesh=mesh,
        in_specs=(
            P(("dp", "tensor"), None),
            P("dp", "tensor"),
            P("dp", "tensor"),
            P("dp", "tensor"),
            P("dp", "tensor"),
        ),
        out_specs=(P("dp", "tensor"), P("dp", "tensor"), P("dp", "tensor"), P(None, "tensor")),
        check_vma=False,
    )
```

```python
import functools

import jax
import jax.numpy as jnp
from jax import lax
from jax.experimental import pallas as pl
from jax.experimental.pallas import tpu as pltpu
from jax.sharding import PartitionSpec as P

first_bias = 0.9999734386011124
second_bias = 0.0952078528862911

SIDE = 4


def device_at(x, y, core):
    return ((x % SIDE) * SIDE + (y % SIDE)) * 2 + core


PLACES = [(x, y, core) for x in range(SIDE) for y in range(SIDE) for core in range(2)]
CORE_SWAP = [(device_at(x, y, core), device_at(x, y, 1 - core)) for x, y, core in PLACES]


def ring(step, along_x_on):
    return [
        (
            device_at(x, y, core),
            device_at(x + step, y, core) if core == along_x_on else device_at(x, y + step, core),
        )
        for x, y, core in PLACES
    ]


def groups(along_x_on):
    lines = []
    for at in range(SIDE):
        lines.append([device_at(i, at, along_x_on) for i in range(SIDE)])
        lines.append([device_at(at, i, 1 - along_x_on) for i in range(SIDE)])
    return lines


def place():
    dp = lax.axis_index("dp")
    return dp // (2 * SIDE), (dp // 2) % SIDE, dp % 2


def block_of(x, y, core, split, reduce):
    first = core == 0
    bx = lax.rem(x + jnp.where(first, split, reduce), SIDE)
    by = lax.rem(y + jnp.where(first, reduce, split), SIDE)
    return (bx * SIDE + by) * 2 + core


def block_at(array, block, rows):
    return array[:, pl.ds(pl.multiple_of(block * rows, rows), rows)]


def blocks_kernel(rows, acts, *outs):
    x, y, core = place()
    for split in range(SIDE):
        for reduce in range(SIDE):
            at = slice(reduce * rows, (reduce + 1) * rows)
            outs[split][:, at] = block_at(acts, block_of(x, y, core, split, reduce), rows)
            outs[SIDE + split][:, at] = block_at(acts, block_of(x, y, 1 - core, split, reduce), rows)


def product_kernel(which, rows, *refs):
    acts, grads, outs = refs[: 2 * SIDE], refs[2 * SIDE : 4 * SIDE], refs[4 * SIDE :]
    panels = grads[0].shape[0]
    here = lax.axis_index("tensor")
    left = {
        reduce: jnp.concatenate(
            [piece[:, reduce * rows : (reduce + 1) * rows].T for piece in acts], axis=1
        )
        for reduce in sorted({reduce for reduce, _ in which})
    }
    for (reduce, away), out in zip(which, outs):
        for i, step in enumerate(away):
            panel = lax.rem(here + step, panels)
            right = jnp.concatenate([piece[panel] for piece in grads], axis=0)
            out[i] = jnp.dot(left[reduce], right, preferred_element_type=jnp.float32).astype(out.dtype)


def weights_kernel(*refs):
    *parts, out = refs
    x, y, core = place()
    panel_x = pl.program_id(0)
    off_x = lax.rem(x + SIDE - panel_x, SIDE)
    for of_core in range(2):
        first, second = parts[SIDE * of_core :][:SIDE], parts[SIDE * (1 - of_core) :][:SIDE]

        for case in range(SIDE):

            @pl.when((core == of_core) & (y == case))
            def _():
                for at in range(SIDE):
                    out[0, at, 0] = first[(case - at) % SIDE][off_x]

            @pl.when((core == of_core) & (off_x == case))
            def _():
                for at in range(SIDE):
                    out[0, at, 1] = second[case][lax.rem(y + SIDE - at, SIDE)]


VMEM = pl.BlockSpec(memory_space=pltpu.VMEM)


def mover(kernel, out_shape, inputs):
    return pl.pallas_call(
        kernel,
        out_shape=out_shape,
        in_specs=[VMEM] * inputs,
        out_specs=jax.tree.map(lambda _: VMEM, out_shape),
        compiler_params=pltpu.CompilerParams(vmem_limit_bytes=20 * 1024 * 1024),
    )


def per_device(activations, out_grads, master, first_moment, second_moment):
    tokens, width = activations.shape
    rows, cols = master.shape
    panels = out_grads.shape[0] // tokens
    kept = jax.ShapeDtypeStruct
    wide = SIDE * rows

    chunk = kept((tokens, wide), jnp.bfloat16)
    chunks = mover(functools.partial(blocks_kernel, rows), [chunk] * (2 * SIDE), 1)(activations)
    from_peer = [lax.ppermute(part, "dp", CORE_SWAP) for part in chunks[SIDE:]]
    acts = [
        part[i] if i == 0 else lax.ppermute(part[i], "dp", ring(i, 0))
        for part in (chunks[:SIDE], from_peer)
        for i in range(SIDE)
    ]

    mine = lax.all_to_all(out_grads.reshape(panels, tokens, cols), "tensor", 0, 0)
    mine, acts = lax.optimization_barrier((mine, acts))
    peer = lax.ppermute(mine, "dp", CORE_SWAP)
    grads = [
        part if i == 0 else lax.ppermute(part, "dp", ring(i, 0)) for part in (mine, peer) for i in range(SIDE)
    ]

    def product(*which):
        return mover(
            functools.partial(product_kernel, which, rows),
            [kept((len(away), rows, cols), jnp.bfloat16) for _, away in which],
            4 * SIDE,
        )(*acts, *grads)

    far = (panels // 2, panels // 2 - 1, panels // 2 + 1)
    near = tuple(step for step in range(panels) if step not in far)
    f32 = jnp.float32
    moved = [
        [lax.ppermute(part, "dp", ring(i, 1)) for i, part in zip((2, 1, 3), product((2, away), (1, away), (3, away)))]
        for away in (far, near)
    ]
    kept_parts = product((0, far), (0, near))

    def line(at):
        return sum((part.astype(f32) for part in moved[at]), kept_parts[at].astype(f32)).astype(jnp.bfloat16)

    def along_tensor(part, step):
        return lax.ppermute(part, "tensor", [(i, (i + step) % panels) for i in range(panels)])

    line_far = line(0)
    terms = [along_tensor(line_far[i], step) for i, step in enumerate(far)]
    line_near = line(1)
    terms += [along_tensor(line_near[i], step) for i, step in enumerate(near) if step]
    grad = sum((term.astype(f32) for term in terms), line_near[0].astype(f32))

    new_first = 0.9 * first_moment + 0.1 * grad
    new_second = 0.999 * second_moment + 0.001 * grad * grad
    first_fix = new_first / first_bias
    second_fix = new_second / second_bias
    new_master = master * (1.0 - 0.05 * 0.1) - 0.05 * first_fix / (jnp.sqrt(second_fix) + 1e-08)

    own = new_master.astype(jnp.bfloat16)
    line = jnp.stack([own] + [lax.ppermute(own, "dp", ring(i, 0)) for i in range(1, SIDE)])
    own = [line] + [lax.ppermute(line, "dp", ring(i, 1)) for i in range(1, SIDE)]
    peer = [lax.ppermute(part, "dp", CORE_SWAP) for part in own]
    weights = pl.pallas_call(
        weights_kernel,
        grid=(SIDE,),
        out_shape=kept((SIDE, SIDE, 2, rows, cols), jnp.bfloat16),
        in_specs=[VMEM] * (2 * SIDE),
        out_specs=pl.BlockSpec((1, SIDE, 2, rows, cols), lambda i: (i, 0, 0, 0, 0)),
        compiler_params=pltpu.CompilerParams(vmem_limit_bytes=20 * 1024 * 1024),
    )(*own, *peer).reshape(width, cols)
    return (new_master, new_first, new_second, weights)


def solution(mesh):
    return jax.shard_map(
        per_device,
        mesh=mesh,
        in_specs=(
            P(("dp", "tensor"), None),
            P("dp", "tensor"),
            P("dp", "tensor"),
            P("dp", "tensor"),
            P("dp", "tensor"),
        ),
        out_specs=(P("dp", "tensor"), P("dp", "tensor"), P("dp", "tensor"), P(None, "tensor")),
        check_vma=False,
    )
```

```python
import functools

import jax
import jax.numpy as jnp
from jax import lax
from jax.experimental import pallas as pl
from jax.experimental.pallas import tpu as pltpu
from jax.sharding import PartitionSpec as P

first_bias = 0.9999734386011124
second_bias = 0.0952078528862911

SIDE = 4


def device_at(x, y, core):
    return ((x % SIDE) * SIDE + (y % SIDE)) * 2 + core


PLACES = [(x, y, core) for x in range(SIDE) for y in range(SIDE) for core in range(2)]
CORE_SWAP = [(device_at(x, y, core), device_at(x, y, 1 - core)) for x, y, core in PLACES]


def ring(step, along_x_on):
    return [
        (
            device_at(x, y, core),
            device_at(x + step, y, core) if core == along_x_on else device_at(x, y + step, core),
        )
        for x, y, core in PLACES
    ]


def groups(along_x_on):
    lines = []
    for at in range(SIDE):
        lines.append([device_at(i, at, along_x_on) for i in range(SIDE)])
        lines.append([device_at(at, i, 1 - along_x_on) for i in range(SIDE)])
    return lines


def place():
    dp = lax.axis_index("dp")
    return dp // (2 * SIDE), (dp // 2) % SIDE, dp % 2


def block_of(x, y, core, split, reduce):
    first = core == 0
    bx = lax.rem(x + jnp.where(first, split, reduce), SIDE)
    by = lax.rem(y + jnp.where(first, reduce, split), SIDE)
    return (bx * SIDE + by) * 2 + core


def block_at(array, block, rows):
    return array[:, pl.ds(pl.multiple_of(block * rows, rows), rows)]


def blocks_kernel(rows, acts, *outs):
    x, y, core = place()
    for split in range(SIDE):
        for reduce in range(SIDE):
            at = slice(reduce * rows, (reduce + 1) * rows)
            outs[split][:, at] = block_at(acts, block_of(x, y, core, split, reduce), rows)
            outs[SIDE + split][:, at] = block_at(acts, block_of(x, y, 1 - core, split, reduce), rows)


def product_kernel(which, rows, *refs):
    acts, grads, outs = refs[: 2 * SIDE], refs[2 * SIDE : 4 * SIDE], refs[4 * SIDE :]
    panels = grads[0].shape[0]
    here = lax.axis_index("tensor")
    left = {
        reduce: jnp.concatenate(
            [piece[:, reduce * rows : (reduce + 1) * rows].T for piece in acts], axis=1
        )
        for reduce in sorted({reduce for reduce, _ in which})
    }
    for (reduce, away), out in zip(which, outs):
        for i, step in enumerate(away):
            panel = lax.rem(here + step, panels)
            right = jnp.concatenate([piece[panel] for piece in grads], axis=0)
            out[i] = jnp.dot(left[reduce], right, preferred_element_type=jnp.float32).astype(out.dtype)


def weights_kernel(*refs):
    *parts, out = refs
    x, y, core = place()
    panel_x = pl.program_id(0)
    off_x = lax.rem(x + SIDE - panel_x, SIDE)
    for of_core in range(2):
        first, second = parts[SIDE * of_core :][:SIDE], parts[SIDE * (1 - of_core) :][:SIDE]

        for case in range(SIDE):

            @pl.when((core == of_core) & (y == case))
            def _():
                for at in range(SIDE):
                    out[0, at, 0] = first[(case - at) % SIDE][off_x]

            @pl.when((core == of_core) & (off_x == case))
            def _():
                for at in range(SIDE):
                    out[0, at, 1] = second[case][lax.rem(y + SIDE - at, SIDE)]


VMEM = pl.BlockSpec(memory_space=pltpu.VMEM)


def mover(kernel, out_shape, inputs):
    return pl.pallas_call(
        kernel,
        out_shape=out_shape,
        in_specs=[VMEM] * inputs,
        out_specs=jax.tree.map(lambda _: VMEM, out_shape),
        compiler_params=pltpu.CompilerParams(vmem_limit_bytes=20 * 1024 * 1024),
    )


def per_device(activations, out_grads, master, first_moment, second_moment):
    tokens, width = activations.shape
    rows, cols = master.shape
    panels = out_grads.shape[0] // tokens
    kept = jax.ShapeDtypeStruct
    wide = SIDE * rows

    chunk = kept((tokens, wide), jnp.bfloat16)
    chunks = mover(functools.partial(blocks_kernel, rows), [chunk] * (2 * SIDE), 1)(activations)
    from_peer = [lax.ppermute(part, "dp", CORE_SWAP) for part in chunks[SIDE:]]
    acts = [
        part[i] if i == 0 else lax.ppermute(part[i], "dp", ring(i, 0))
        for part in (chunks[:SIDE], from_peer)
        for i in range(SIDE)
    ]

    mine = lax.all_to_all(out_grads.reshape(panels, tokens, cols), "tensor", 0, 0)
    mine, acts = lax.optimization_barrier((mine, acts))
    peer = lax.ppermute(mine, "dp", CORE_SWAP)
    up, down = lax.ppermute(mine, "dp", ring(1, 0)), lax.ppermute(mine, "dp", ring(3, 0))
    grads = [mine, up, lax.ppermute(up, "dp", ring(1, 0)), down]
    up, down = lax.ppermute(peer, "dp", ring(1, 0)), lax.ppermute(peer, "dp", ring(3, 0))
    grads += [peer, up, lax.ppermute(down, "dp", ring(3, 0)), down]

    def product(*which):
        return mover(
            functools.partial(product_kernel, which, rows),
            [kept((len(away), rows, cols), jnp.bfloat16) for _, away in which],
            4 * SIDE,
        )(*acts, *grads)

    far = (panels // 2, panels // 2 - 1, panels // 2 + 1)
    near = tuple(step for step in range(panels) if step not in far)
    f32 = jnp.float32
    moved = [
        [lax.ppermute(part, "dp", ring(i, 1)) for i, part in zip((2, 1, 3), product((2, away)) + product((1, away), (3, away)))]
        for away in (far, near)
    ]
    kept_parts = product((0, far), (0, near))

    def line(at):
        return sum((part.astype(f32) for part in moved[at]), kept_parts[at].astype(f32))

    def along_tensor(part, step):
        return lax.ppermute(part, "tensor", [(i, (i + step) % panels) for i in range(panels)])

    half = panels // 2
    at_half, at_up, at_down = line(0).astype(jnp.bfloat16)
    joins_up, joins_down = along_tensor(at_up, 1), along_tensor(at_down, panels - 1)
    halfway = along_tensor(at_half, half)
    totals = dict(zip(near, line(1)))
    totals[half // 2] += joins_up.astype(f32)
    totals[panels - half // 2] += joins_down.astype(f32)
    terms = [halfway] + [along_tensor(totals[step].astype(jnp.bfloat16), step) for step in near if step]
    grad = sum((term.astype(f32) for term in terms), totals[0])

    new_first = 0.9 * first_moment + 0.1 * grad
    new_second = 0.999 * second_moment + 0.001 * grad * grad
    first_fix = new_first / first_bias
    second_fix = new_second / second_bias
    new_master = master * (1.0 - 0.05 * 0.1) - 0.05 * first_fix / (jnp.sqrt(second_fix) + 1e-08)

    own = new_master.astype(jnp.bfloat16)
    moved = {i: lax.ppermute(own, "dp", ring(i, 0)) for i in (2, 1, 3)}
    line = jnp.stack([own] + [moved[i] for i in range(1, SIDE)])
    moved = {i: lax.ppermute(line, "dp", ring(i, 1)) for i in (2, 1, 3)}
    own = [line] + [moved[i] for i in range(1, SIDE)]
    peer = [lax.ppermute(part, "dp", CORE_SWAP) for part in own]
    weights = pl.pallas_call(
        weights_kernel,
        grid=(SIDE,),
        out_shape=kept((SIDE, SIDE, 2, rows, cols), jnp.bfloat16),
        in_specs=[VMEM] * (2 * SIDE),
        out_specs=pl.BlockSpec((1, SIDE, 2, rows, cols), lambda i: (i, 0, 0, 0, 0)),
        compiler_params=pltpu.CompilerParams(vmem_limit_bytes=20 * 1024 * 1024),
    )(*own, *peer).reshape(width, cols)
    return (new_master, new_first, new_second, weights)


def solution(mesh):
    return jax.shard_map(
        per_device,
        mesh=mesh,
        in_specs=(
            P(("dp", "tensor"), None),
            P("dp", "tensor"),
            P("dp", "tensor"),
            P("dp", "tensor"),
            P("dp", "tensor"),
        ),
        out_specs=(P("dp", "tensor"), P("dp", "tensor"), P("dp", "tensor"), P(None, "tensor")),
        check_vma=False,
    )
```

```python
import functools

import jax
import jax.numpy as jnp
from jax import lax
from jax.experimental import pallas as pl
from jax.experimental.pallas import tpu as pltpu
from jax.sharding import PartitionSpec as P

first_bias = 0.9999734386011124
second_bias = 0.0952078528862911

SIDE = 4


def device_at(x, y, core):
    return ((x % SIDE) * SIDE + (y % SIDE)) * 2 + core


PLACES = [(x, y, core) for x in range(SIDE) for y in range(SIDE) for core in range(2)]
CORE_SWAP = [(device_at(x, y, core), device_at(x, y, 1 - core)) for x, y, core in PLACES]


def ring(step, along_x_on):
    return [
        (
            device_at(x, y, core),
            device_at(x + step, y, core) if core == along_x_on else device_at(x, y + step, core),
        )
        for x, y, core in PLACES
    ]


def groups(along_x_on):
    lines = []
    for at in range(SIDE):
        lines.append([device_at(i, at, along_x_on) for i in range(SIDE)])
        lines.append([device_at(at, i, 1 - along_x_on) for i in range(SIDE)])
    return lines


def place():
    dp = lax.axis_index("dp")
    return dp // (2 * SIDE), (dp // 2) % SIDE, dp % 2


def block_of(x, y, core, split, reduce):
    first = core == 0
    bx = lax.rem(x + jnp.where(first, split, reduce), SIDE)
    by = lax.rem(y + jnp.where(first, reduce, split), SIDE)
    return (bx * SIDE + by) * 2 + core


def block_at(array, block, rows):
    return array[:, pl.ds(pl.multiple_of(block * rows, rows), rows)]


def blocks_kernel(rows, acts, *outs):
    x, y, core = place()
    for split in range(SIDE):
        for reduce in range(SIDE):
            at = slice(reduce * rows, (reduce + 1) * rows)
            outs[split][:, at] = block_at(acts, block_of(x, y, core, split, reduce), rows)
            outs[SIDE + split][:, at] = block_at(acts, block_of(x, y, 1 - core, split, reduce), rows)


def product_kernel(which, rows, *refs):
    acts, grads, outs = refs[: 2 * SIDE], refs[2 * SIDE : 4 * SIDE], refs[4 * SIDE :]
    panels = grads[0].shape[0]
    here = lax.axis_index("tensor")
    left = {
        reduce: jnp.concatenate(
            [piece[:, reduce * rows : (reduce + 1) * rows].T for piece in acts], axis=1
        )
        for reduce in sorted({reduce for reduce, _ in which})
    }
    for (reduce, away), out in zip(which, outs):
        for i, step in enumerate(away):
            panel = lax.rem(here + step, panels)
            right = jnp.concatenate([piece[panel] for piece in grads], axis=0)
            out[i] = jnp.dot(left[reduce], right, preferred_element_type=jnp.float32).astype(out.dtype)


def weights_kernel(*refs):
    *parts, out = refs
    x, y, core = place()
    panel_x = pl.program_id(0)
    off_x = lax.rem(x + SIDE - panel_x, SIDE)
    for of_core in range(2):
        first, second = parts[SIDE * of_core :][:SIDE], parts[SIDE * (1 - of_core) :][:SIDE]

        for case in range(SIDE):

            @pl.when((core == of_core) & (y == case))
            def _():
                for at in range(SIDE):
                    out[0, at, 0] = first[(case - at) % SIDE][off_x]

            @pl.when((core == of_core) & (off_x == case))
            def _():
                for at in range(SIDE):
                    out[0, at, 1] = second[case][lax.rem(y + SIDE - at, SIDE)]


VMEM = pl.BlockSpec(memory_space=pltpu.VMEM)


def mover(kernel, out_shape, inputs):
    return pl.pallas_call(
        kernel,
        out_shape=out_shape,
        in_specs=[VMEM] * inputs,
        out_specs=jax.tree.map(lambda _: VMEM, out_shape),
        compiler_params=pltpu.CompilerParams(vmem_limit_bytes=20 * 1024 * 1024),
    )


def per_device(activations, out_grads, master, first_moment, second_moment):
    tokens, width = activations.shape
    rows, cols = master.shape
    panels = out_grads.shape[0] // tokens
    kept = jax.ShapeDtypeStruct
    wide = SIDE * rows

    chunk = kept((tokens, wide), jnp.bfloat16)
    chunks = mover(functools.partial(blocks_kernel, rows), [chunk] * (2 * SIDE), 1)(activations)
    from_peer = [lax.ppermute(part, "dp", CORE_SWAP) for part in chunks[SIDE:]]
    acts = [
        part[i] if i == 0 else lax.ppermute(part[i], "dp", ring(i, 0))
        for part in (chunks[:SIDE], from_peer)
        for i in range(SIDE)
    ]

    mine = lax.all_to_all(out_grads.reshape(panels, tokens, cols), "tensor", 0, 0)
    early = (2, 6, 1, 3)
    mine, first = lax.optimization_barrier((mine, [acts[i] for i in early]))
    for i, part in zip(early, first):
        acts[i] = part
    peer = lax.ppermute(mine, "dp", CORE_SWAP)
    up, down = lax.ppermute(mine, "dp", ring(1, 0)), lax.ppermute(mine, "dp", ring(3, 0))
    grads = [mine, up, lax.ppermute(up, "dp", ring(1, 0)), down]
    up, down = lax.ppermute(peer, "dp", ring(1, 0)), lax.ppermute(peer, "dp", ring(3, 0))
    grads += [peer, up, lax.ppermute(down, "dp", ring(3, 0)), down]

    def product(*which):
        return mover(
            functools.partial(product_kernel, which, rows),
            [kept((len(away), rows, cols), jnp.bfloat16) for _, away in which],
            4 * SIDE,
        )(*acts, *grads)

    far = (panels // 2, panels // 2 - 1, panels // 2 + 1)
    near = tuple(step for step in range(panels) if step not in far)
    f32 = jnp.float32
    moved = [
        [lax.ppermute(part, "dp", ring(i, 1)) for i, part in zip((2, 1, 3), product((2, away)) + product((1, away), (3, away)))]
        for away in (far, near)
    ]
    kept_parts = product((0, far), (0, near))

    def line(at):
        return sum((part.astype(f32) for part in moved[at]), kept_parts[at].astype(f32))

    def along_tensor(part, step):
        return lax.ppermute(part, "tensor", [(i, (i + step) % panels) for i in range(panels)])

    half = panels // 2
    at_half, at_up, at_down = line(0).astype(jnp.bfloat16)
    joins_up, joins_down = along_tensor(at_up, 1), along_tensor(at_down, panels - 1)
    halfway = along_tensor(at_half, half)
    totals = dict(zip(near, line(1)))
    totals[half // 2] += joins_up.astype(f32)
    totals[panels - half // 2] += joins_down.astype(f32)
    terms = [halfway] + [along_tensor(totals[step].astype(jnp.bfloat16), step) for step in near if step]
    grad = sum((term.astype(f32) for term in terms), totals[0])

    new_first = 0.9 * first_moment + 0.1 * grad
    new_second = 0.999 * second_moment + 0.001 * grad * grad
    first_fix = new_first / first_bias
    second_fix = new_second / second_bias
    new_master = master * (1.0 - 0.05 * 0.1) - 0.05 * first_fix / (jnp.sqrt(second_fix) + 1e-08)

    own = new_master.astype(jnp.bfloat16)
    moved = {i: lax.ppermute(own, "dp", ring(i, 0)) for i in (2, 1, 3)}
    line = jnp.stack([own] + [moved[i] for i in range(1, SIDE)])
    moved = {i: lax.ppermute(line, "dp", ring(i, 1)) for i in (2, 1, 3)}
    own = [line] + [moved[i] for i in range(1, SIDE)]
    peer = [lax.ppermute(part, "dp", CORE_SWAP) for part in own]
    weights = pl.pallas_call(
        weights_kernel,
        grid=(SIDE,),
        out_shape=kept((SIDE, SIDE, 2, rows, cols), jnp.bfloat16),
        in_specs=[VMEM] * (2 * SIDE),
        out_specs=pl.BlockSpec((1, SIDE, 2, rows, cols), lambda i: (i, 0, 0, 0, 0)),
        compiler_params=pltpu.CompilerParams(vmem_limit_bytes=20 * 1024 * 1024),
    )(*own, *peer).reshape(width, cols)
    return (new_master, new_first, new_second, weights)


def solution(mesh):
    return jax.shard_map(
        per_device,
        mesh=mesh,
        in_specs=(
            P(("dp", "tensor"), None),
            P("dp", "tensor"),
            P("dp", "tensor"),
            P("dp", "tensor"),
            P("dp", "tensor"),
        ),
        out_specs=(P("dp", "tensor"), P("dp", "tensor"), P("dp", "tensor"), P(None, "tensor")),
        check_vma=False,
    )
```

```python
import functools

import jax
import jax.numpy as jnp
from jax import lax
from jax.experimental import pallas as pl
from jax.experimental.pallas import tpu as pltpu
from jax.sharding import PartitionSpec as P

first_bias = 0.9999734386011124
second_bias = 0.0952078528862911

SIDE = 4


def device_at(x, y, core):
    return ((x % SIDE) * SIDE + (y % SIDE)) * 2 + core


PLACES = [(x, y, core) for x in range(SIDE) for y in range(SIDE) for core in range(2)]
CORE_SWAP = [(device_at(x, y, core), device_at(x, y, 1 - core)) for x, y, core in PLACES]


def ring(step, along_x_on):
    return [
        (
            device_at(x, y, core),
            device_at(x + step, y, core) if core == along_x_on else device_at(x, y + step, core),
        )
        for x, y, core in PLACES
    ]


def groups(along_x_on):
    lines = []
    for at in range(SIDE):
        lines.append([device_at(i, at, along_x_on) for i in range(SIDE)])
        lines.append([device_at(at, i, 1 - along_x_on) for i in range(SIDE)])
    return lines


def place():
    dp = lax.axis_index("dp")
    return dp // (2 * SIDE), (dp // 2) % SIDE, dp % 2


def block_of(x, y, core, split, reduce):
    first = core == 0
    bx = lax.rem(x + jnp.where(first, split, reduce), SIDE)
    by = lax.rem(y + jnp.where(first, reduce, split), SIDE)
    return (bx * SIDE + by) * 2 + core


def block_at(array, block, rows):
    return array[:, pl.ds(pl.multiple_of(block * rows, rows), rows)]


def blocks_kernel(rows, acts, *outs):
    x, y, core = place()
    for split in range(SIDE):
        for reduce in range(SIDE):
            at = slice(reduce * rows, (reduce + 1) * rows)
            outs[split][:, at] = block_at(acts, block_of(x, y, core, split, reduce), rows)
            outs[SIDE + split][:, at] = block_at(acts, block_of(x, y, 1 - core, split, reduce), rows)


def product_kernel(which, rows, *refs):
    acts, grads, outs = refs[: 2 * SIDE], refs[2 * SIDE : 4 * SIDE], refs[4 * SIDE :]
    panels = grads[0].shape[0]
    here = lax.axis_index("tensor")
    left = {
        reduce: jnp.concatenate(
            [piece[:, reduce * rows : (reduce + 1) * rows].T for piece in acts], axis=1
        )
        for reduce in sorted({reduce for reduce, _ in which})
    }
    for (reduce, away), out in zip(which, outs):
        for i, step in enumerate(away):
            panel = lax.rem(here + step, panels)
            right = jnp.concatenate([piece[panel] for piece in grads], axis=0)
            out[i] = jnp.dot(left[reduce], right, preferred_element_type=jnp.float32).astype(out.dtype)


def weights_kernel(*refs):
    *parts, out = refs
    x, y, core = place()
    panel_x = pl.program_id(0)
    off_x = lax.rem(x + SIDE - panel_x, SIDE)
    for of_core in range(2):
        first, second = parts[SIDE * of_core :][:SIDE], parts[SIDE * (1 - of_core) :][:SIDE]

        for case in range(SIDE):

            @pl.when((core == of_core) & (y == case))
            def _():
                for at in range(SIDE):
                    out[0, at, 0] = first[(case - at) % SIDE][off_x]

            @pl.when((core == of_core) & (off_x == case))
            def _():
                for at in range(SIDE):
                    out[0, at, 1] = second[case][lax.rem(y + SIDE - at, SIDE)]


VMEM = pl.BlockSpec(memory_space=pltpu.VMEM)


def mover(kernel, out_shape, inputs):
    return pl.pallas_call(
        kernel,
        out_shape=out_shape,
        in_specs=[VMEM] * inputs,
        out_specs=jax.tree.map(lambda _: VMEM, out_shape),
        compiler_params=pltpu.CompilerParams(vmem_limit_bytes=20 * 1024 * 1024),
    )


def per_device(activations, out_grads, master, first_moment, second_moment):
    tokens, width = activations.shape
    rows, cols = master.shape
    panels = out_grads.shape[0] // tokens
    kept = jax.ShapeDtypeStruct
    wide = SIDE * rows

    chunk = kept((tokens, wide), jnp.bfloat16)
    chunks = mover(functools.partial(blocks_kernel, rows), [chunk] * (2 * SIDE), 1)(activations)
    from_peer = [lax.ppermute(part, "dp", CORE_SWAP) for part in chunks[SIDE:]]
    acts = []
    for part in (chunks[:SIDE], from_peer):
        sent = {i: lax.ppermute(part[i], "dp", ring(i, 0)) for i in (2, 1, 3)}
        acts += [part[0]] + [sent[i] for i in range(1, SIDE)]

    mine = lax.all_to_all(out_grads.reshape(panels, tokens, cols), "tensor", 0, 0)
    early = (2, 6, 1, 3)
    mine, first = lax.optimization_barrier((mine, [acts[i] for i in early]))
    for i, part in zip(early, first):
        acts[i] = part
    peer = lax.ppermute(mine, "dp", CORE_SWAP)
    up, down = lax.ppermute(mine, "dp", ring(1, 0)), lax.ppermute(mine, "dp", ring(3, 0))
    grads = [mine, up, lax.ppermute(up, "dp", ring(1, 0)), down]
    up, down = lax.ppermute(peer, "dp", ring(1, 0)), lax.ppermute(peer, "dp", ring(3, 0))
    grads += [peer, up, lax.ppermute(down, "dp", ring(3, 0)), down]

    def product(*which):
        return mover(
            functools.partial(product_kernel, which, rows),
            [kept((len(away), rows, cols), jnp.bfloat16) for _, away in which],
            4 * SIDE,
        )(*acts, *grads)

    far = (panels // 2, panels // 2 - 1, panels // 2 + 1)
    near = tuple(step for step in range(panels) if step not in far)
    f32 = jnp.float32
    moved = [
        [lax.ppermute(part, "dp", ring(i, 1)) for i, part in zip((2, 1, 3), product((2, away)) + product((1, away), (3, away)))]
        for away in (far, near)
    ]
    kept_parts = product((0, far), (0, near))

    def line(at):
        return sum((part.astype(f32) for part in moved[at]), kept_parts[at].astype(f32))

    def along_tensor(part, step):
        return lax.ppermute(part, "tensor", [(i, (i + step) % panels) for i in range(panels)])

    half = panels // 2
    at_half, at_up, at_down = line(0).astype(jnp.bfloat16)
    joins_up, joins_down = along_tensor(at_up, 1), along_tensor(at_down, panels - 1)
    halfway = along_tensor(at_half, half)
    totals = dict(zip(near, line(1)))
    totals[half // 2] += joins_up.astype(f32)
    totals[panels - half // 2] += joins_down.astype(f32)
    terms = [halfway] + [along_tensor(totals[step].astype(jnp.bfloat16), step) for step in near if step]
    grad = sum((term.astype(f32) for term in terms), totals[0])

    new_first = 0.9 * first_moment + 0.1 * grad
    new_second = 0.999 * second_moment + 0.001 * grad * grad
    first_fix = new_first / first_bias
    second_fix = new_second / second_bias
    new_master = master * (1.0 - 0.05 * 0.1) - 0.05 * first_fix / (jnp.sqrt(second_fix) + 1e-08)

    own = new_master.astype(jnp.bfloat16)
    moved = {i: lax.ppermute(own, "dp", ring(i, 0)) for i in (2, 1, 3)}
    line = jnp.stack([own] + [moved[i] for i in range(1, SIDE)])
    moved = {i: lax.ppermute(line, "dp", ring(i, 1)) for i in (2, 1, 3)}
    own = [line] + [moved[i] for i in range(1, SIDE)]
    peer = [lax.ppermute(part, "dp", CORE_SWAP) for part in own]
    weights = pl.pallas_call(
        weights_kernel,
        grid=(SIDE,),
        out_shape=kept((SIDE, SIDE, 2, rows, cols), jnp.bfloat16),
        in_specs=[VMEM] * (2 * SIDE),
        out_specs=pl.BlockSpec((1, SIDE, 2, rows, cols), lambda i: (i, 0, 0, 0, 0)),
        compiler_params=pltpu.CompilerParams(vmem_limit_bytes=20 * 1024 * 1024),
    )(*own, *peer).reshape(width, cols)
    return (new_master, new_first, new_second, weights)


def solution(mesh):
    return jax.shard_map(
        per_device,
        mesh=mesh,
        in_specs=(
            P(("dp", "tensor"), None),
            P("dp", "tensor"),
            P("dp", "tensor"),
            P("dp", "tensor"),
            P("dp", "tensor"),
        ),
        out_specs=(P("dp", "tensor"), P("dp", "tensor"), P("dp", "tensor"), P(None, "tensor")),
        check_vma=False,
    )
```
